32 devices in a mesh: rows: 8 (over z, y), dp: 4 (over x, core).
Axes of the slice: x: 2, y: 2, z: 4, core: 2. Of those that a mesh axis runs over, the one named last changes fastest.
Arguments:
- tokens: bfloat16 [16384, 512], P(('rows', 'dp')), may hold values from -6 to 6
- out_grad: bfloat16 [16384, 512], P(('rows', 'dp')), may hold values from -6 to 6
- seq_lengths: int32 [32, 4], P(('rows', 'dp')), may hold values from 1 to 256, 512 in all within a row
- owners: int32 [16384, 1], P(('rows', 'dp')), may hold values from 0 to 7; in each aligned block of 512 rows (0 to 511, 512 to 1023, ...) at most 256 rows name the same one
- slots: int32 [16384], P(('rows', 'dp')), may hold values from 0 to 127
- w_in: bfloat16 [512, 1024], replicated, may hold values from -0.25 to 0.25
- w_out: bfloat16 [512, 256], replicated, may hold values from -0.375 to 0.375
- emb_rows: float32 [1024, 512], P('rows'), may hold values from -0.6 to 0.6
- emb_mom: float32 [1024, 512], P('rows'), may hold values from -0.6 to 0.6
- emb_var: float32 [1024], P('rows'), may hold values from 0.01 to 0.1
Outputs:
- new_rows: float32 [1024, 512], P('rows')
- new_mom: float32 [1024, 512], P('rows')
- new_var: float32 [1024], P('rows')
- w_in_grad: float32 [512, 1024], P('rows')
- w_out_grad: float32 [512, 256], P('rows')
The draws below stay inside these ranges and needn't reach their ends.
Inputs may be any that keep to these rules, and one draw needn't show every extreme that they name: `seq_lengths`: each row sums to 512; its largest entry is exactly 256. `owners`: among the 512 tokens of one device at most 256 name the same owner; some device reaches 256.
All inputs are finite; a program needn't handle non-finite values.
Results may differ from the reference program's by a relative error of at most 0.015.
Values may be sent and summed in bfloat16 or wider, within the bound.
A program may use at most 64 MiB of HBM per device.

```python
import math
import jax
import jax.numpy as jnp
import numpy as np
from jax import lax

D = 512
HEADS = 4
HEAD_DIM = 64
HW = 256
TOK_DEV = 512
NSEQ = 4
MAXLEN = 256
SLOTS = 128
CAP = 256
TOKENS = 16384
TABLE = 1024
N_ROWS = 8
DEVICES = 32


def touch_ends(array, own_key, low, largest):
    shape = array.shape
    spot = [jax.random.randint(jax.random.fold_in(own_key, axis), (), 0, shape[axis]) for axis in range(len(shape))]
    array = array.at[tuple(spot)].set(low)
    longest = shape.index(max(shape))
    spot[longest] = (spot[longest] + 1) % shape[longest]
    return array.at[tuple(spot)].set(largest)


def with_spikes(drawn, key, source, target, blocks, factor):
    owner, partner = [(jnp.arange(drawn.shape[dim]) // (drawn.shape[dim] // blocks)).reshape([-1 if axis == dim else 1 for axis in range(drawn.ndim)]) for dim in (source, target)]
    chosen = jax.random.permutation(key, blocks)[partner]
    strong = (owner == chosen) | (owner == (partner + blocks // 2) % blocks)
    return jnp.where(strong, factor * drawn, drawn)


def block_levels(own_key, shape, cuts, low, largest):
    loudness, own = 1.0, jax.random.fold_in(own_key, 6)
    for dim, shards_of in cuts:
        heights = jnp.exp(jax.random.uniform(jax.random.fold_in(own, dim), (shards_of,), jnp.float32, low / len(cuts), largest / len(cuts)))
        loudness = loudness * jnp.repeat(heights, shape[dim] // shards_of).reshape([-1 if axis == dim else 1 for axis in range(len(shape))])
    return loudness


def rank_table(number_of, slope):
    loads = [(1 << 20) // math.isqrt(rank ** slope) + 1 for rank in range(1, number_of + 1)]
    scale = 1 + sum(loads) // (1 << 30)
    return np.cumsum(np.array([max(1, weight // scale) for weight in loads]))


def ranked(rng, shape, amount, skew):
    table = rank_table(amount, skew)
    lot = jax.random.randint(jax.random.fold_in(rng, 1), shape, 0, int(table[amount - 1]))
    standing = jnp.searchsorted(jnp.asarray(table, jnp.int32), lot, side="right")
    return jax.random.permutation(jax.random.fold_in(rng, 2), amount)[standing].astype(jnp.int32)


def profile(amount, total, reach, lean):
    loads = [(1 << 20) // math.isqrt(standing ** lean) + 1 for standing in range(2, amount + 1)]
    surplus, given = total - reach - (amount - 1), [1] * (amount - 1)
    while surplus > 0:
        free = [i for i in range(amount - 1) if given[i] < reach]
        pool, left = sum([loads[i] for i in free]), surplus
        for i in free:
            extra = min(reach - given[i], max(1, left * loads[i] // pool), surplus)
            given[i] = given[i] + extra
            surplus = surplus - extra
    return np.array([reach] + given)


def ragged_sizes(key, count, total, bound, slope):
    if count == 2:
        one = jax.random.randint(key, (), max(1, total - bound), min(bound, total - 1) + 1)
        return jnp.stack([one, total - one])
    sizes = jnp.asarray(profile(count, total, bound, slope), jnp.int32)
    pairs = (count - 1) // 2
    source_of, taker = sizes[1:1 + 2 * pairs:2], sizes[2:2 + 2 * pairs:2]
    margin = jnp.minimum(source_of - 1, bound - taker)
    moved = jax.random.randint(jax.random.fold_in(key, 1), (pairs,), 0, 1 << 20) % (margin + 1)
    sizes = sizes.at[1:1 + 2 * pairs:2].set(source_of - moved).at[2:2 + 2 * pairs:2].set(taker + moved)
    return sizes[jax.random.permutation(jax.random.fold_in(key, 2), count)]


def routed_block(own_key, own, number, rows, number_of, top, most, skew):
    order = jax.random.permutation(own_key, number_of)
    heavy_load, usual = portions_of(number_of, rows * top, most, skew, True), portions_of(number_of, rows * top, most, skew, False)
    places = jnp.arange(number_of)

    def named(sizes, rotation):
        used = int((sizes > 0).sum())
        fixed = max(1, used // 4)
        shifted = fixed + (places - fixed + rotation * (used - fixed)) % max(1, number_of - fixed)
        return jnp.zeros((number_of,), jnp.int32).at[order[jnp.where(places < fixed, places, shifted)]].set(jnp.asarray(sizes, jnp.int32))

    sizes = jnp.where(number % 4 == 0, named(heavy_load, number // 4), named(usual, number - number // 4 - 1))
    mixed = jax.random.permutation(jax.random.fold_in(own, 3), number_of)
    donor, sink = mixed[0:number_of // 2 * 2:2], mixed[1:number_of // 2 * 2:2]
    margin = jnp.minimum(sizes[donor] - 1, most - sizes[sink]) // 2
    margin = jnp.where((donor == order[0]) | (sink == order[0]) | (sizes[sink] == 0), 0, jnp.maximum(margin, 0))
    shifted = jax.random.randint(jax.random.fold_in(own, 4), (number_of // 2,), 0, 1 << 20) % (margin + 1)
    sizes = sizes.at[donor].add(-shifted).at[sink].add(shifted)
    labels = jnp.searchsorted(jnp.cumsum(sizes), jnp.arange(rows * top), side="right").astype(jnp.int32)
    listing = labels.reshape(top, rows).T
    listing = listing[jax.random.permutation(jax.random.fold_in(own, 1), rows)]
    rotation = jax.random.randint(jax.random.fold_in(own, 2), (rows, 1), 0, top)
    return jnp.take_along_axis(listing, (jnp.arange(top)[None, :] + rotation) % top, axis=1)


def portions_of(number_of, total, bound, skew, full):
    weights = [(1 << 20) // math.isqrt(rank ** skew) + 1 for rank in range(1, number_of + 1)]
    largest = bound if full else min(bound, max(-(-total // number_of), total * weights[0] // sum(weights)))
    least = 1 if total - largest >= number_of - 1 else 0
    holding, surplus = [largest] + [least] * (number_of - 1), total - largest - least * (number_of - 1)
    while surplus > 0:
        movable = [i for i in range(1, number_of) if holding[i] < largest] or [i for i in range(1, number_of) if holding[i] < bound]
        pool, left = sum([weights[i] for i in movable]), surplus
        for i in movable:
            addition = min(bound - holding[i], max(1, left * weights[i] // pool), surplus)
            holding[i] = holding[i] + addition
            surplus = surplus - addition
    return np.array(holding)


def scatter_about(own_key, shape, deviation, bound, pieces=(), kind=jnp.bfloat16):
    factor_of = block_levels(own_key, shape, pieces, -0.22, 0.18) if pieces else 1.0
    entries = jax.random.normal(own_key, shape, jnp.float32) * deviation * factor_of
    return jnp.minimum(jnp.maximum(entries, -bound), bound).astype(kind)


def gaussian_with(stream_key, shape, deviation, most, pieces, heavy, kind=jnp.bfloat16):
    result = deviation * jax.random.normal(stream_key, shape, jnp.float32)
    if pieces:
        result = result * block_levels(stream_key, shape, pieces, -0.22, 0.18)
    return jnp.clip(with_spikes(result, jax.random.fold_in(stream_key, 3), *heavy), -most, most).astype(kind)


def setup_inputs(seed: int = 0) -> dict:
    key_list = jax.random.split(jax.random.key(seed), 11)
    tokens = gaussian_with(key_list[0], (TOKENS, D), 1.0, 6.0, ((0, 32),), (0, 1, 32, 2.75))
    out_grad = gaussian_with(key_list[1], (TOKENS, D), 1.0, 6.0, ((0, 32),), (0, 1, 32, 2.75))
    seq_lengths = jax.vmap(lambda own: ragged_sizes(own, NSEQ, TOK_DEV, MAXLEN, 2))(jax.random.split(key_list[2], DEVICES)).reshape((DEVICES, NSEQ)).astype(jnp.int32)
    owners_keys = jax.random.split(jax.random.fold_in(key_list[3], 1), TOKENS // TOK_DEV)
    owners_turns = jax.random.permutation(jax.random.fold_in(key_list[3], 3), TOKENS // TOK_DEV)
    owners = jax.vmap(lambda own, number: routed_block(jax.random.fold_in(key_list[3], 2), own, number, TOK_DEV, N_ROWS, 1, CAP, 2))(owners_keys, owners_turns).reshape((TOKENS, 1))
    slots = touch_ends(ranked(key_list[4], (TOKENS,), SLOTS, 3), jax.random.fold_in(key_list[4], 3), 0, SLOTS - 1).astype(jnp.int32)
    w_in = scatter_about(key_list[5], (D, 4 * HW), D ** -0.5, 0.25)
    w_out = scatter_about(key_list[6], (D, HW), HW ** -0.5, 0.375)
    emb_rows = scatter_about(key_list[7], (TABLE, D), 0.1, 0.6, ((0, 8),), jnp.float32)
    emb_mom = scatter_about(key_list[8], (TABLE, D), 0.1, 0.6, ((0, 8),), jnp.float32)
    emb_var = jnp.clip(jnp.exp(math.log(0.1) - 2.3025851 * jax.random.uniform(key_list[9], (TABLE,), jnp.float32) ** block_levels(key_list[9], (TABLE,), ((0, 8),), -0.2, 0.2)), 0.01, 0.1)
    return dict(tokens=tokens, out_grad=out_grad, seq_lengths=seq_lengths, owners=owners, slots=slots, w_in=w_in, w_out=w_out, emb_rows=emb_rows, emb_mom=emb_mom, emb_var=emb_var)


norm_eps = 1e-06
beta_one = 0.9
beta_two = 0.99
learn_rate = 0.05
adam_eps = 1e-08
bias_one = 1.0 - 0.9 ** 10
bias_two = 1.0 - 0.99 ** 10

def layer_norm(values):
    average = lax.optimization_barrier(jnp.mean(values, axis=-1, keepdims=True))
    centered = values - average
    spread = lax.optimization_barrier(jnp.mean(centered * centered, axis=-1, keepdims=True))
    return centered * lax.rsqrt(spread + norm_eps)

def allowed_mask(lengths, tok_count):
    ends = jnp.cumsum(lengths.astype(jnp.int32))
    position = jnp.arange(tok_count, dtype=jnp.int32)
    segment = lax.optimization_barrier(jnp.sum((position[:, None] >= ends[None, :]).astype(jnp.int32), axis=1))
    same = segment[:, None] == segment[None, :]
    causal = position[None, :] <= position[:, None]
    return (same & causal).astype(jnp.float32)

def core(pre, allowed):
    tok_count = pre.shape[0]
    proj = jax.nn.silu(pre).astype(jnp.bfloat16)
    upart, vpart, qpart, kpart = jnp.split(proj, 4, axis=1)
    queries = qpart.reshape(tok_count, HEADS, HEAD_DIM).astype(jnp.float32)
    keys_part = kpart.reshape(tok_count, HEADS, HEAD_DIM).astype(jnp.float32)
    values_part = vpart.reshape(tok_count, HEADS, HEAD_DIM).astype(jnp.float32)
    scores = jnp.einsum('thd,shd->hts', queries, keys_part) * HEAD_DIM ** (-0.5)
    weights = (jax.nn.silu(scores) * allowed[None] / MAXLEN).astype(jnp.bfloat16)
    attn = jnp.einsum('hts,shd->thd', weights.astype(jnp.float32), values_part).reshape(tok_count, HW)
    return (layer_norm(attn) * upart.astype(jnp.float32)).astype(jnp.bfloat16)

def device_grads(x_part, grad_part, lengths, w_in, w_out):
    allowed = allowed_mask(lengths, x_part.shape[0])
    normed_exact, norm_back = jax.vjp(layer_norm, x_part.astype(jnp.float32))
    normed = normed_exact.astype(jnp.bfloat16)
    pre = jnp.dot(normed, w_in, preferred_element_type=jnp.float32)
    y_out, core_back = jax.vjp(lambda inner: core(inner, allowed), pre)
    y_grad = jnp.dot(grad_part, w_out, preferred_element_type=jnp.float32).astype(jnp.bfloat16)
    pre_grad = core_back(y_grad)[0]
    pre_grad_b = pre_grad.astype(jnp.bfloat16)
    contract = (((0,), (0,)), ((), ()))
    w_in_term = lax.dot_general(normed, pre_grad_b, contract, preferred_element_type=jnp.float32)
    w_out_term = lax.dot_general(grad_part, y_out, contract, preferred_element_type=jnp.float32)
    normed_grad = lax.dot_general(pre_grad_b, w_in, (((1,), (1,)), ((), ())), preferred_element_type=jnp.float32)
    x_grad = norm_back(normed_grad)[0]
    emb_grad = (x_grad + grad_part.astype(jnp.float32)).astype(jnp.bfloat16)
    return (emb_grad, w_in_term, w_out_term)

def row_adam(rows_now, mom_now, var_now, grad, counts):
    touched = counts > 0.5
    mom_next = beta_one * mom_now + (1.0 - beta_one) * grad
    var_next = beta_two * var_now + (1.0 - beta_two) * lax.optimization_barrier(jnp.mean(grad * grad, axis=1))
    advance = mom_next / bias_one / (jnp.sqrt(var_next / bias_two)[:, None] + adam_eps)
    rows_next = rows_now - learn_rate * advance
    return (jnp.where(touched[:, None], rows_next, rows_now), jnp.where(touched[:, None], mom_next, mom_now), jnp.where(touched, var_next, var_now))

def reference(tokens, out_grad, seq_lengths, owners, slots, w_in, w_out, emb_rows, emb_mom, emb_var):
    x_blocks = tokens.reshape(DEVICES, TOK_DEV, D)
    g_blocks = out_grad.reshape(DEVICES, TOK_DEV, D)

    def advance_block(totals, inputs_now):
        x_part, grad_part, lengths = inputs_now
        emb_grad, w_in_term, w_out_term = device_grads(x_part, grad_part, lengths, w_in, w_out)
        return ((totals[0] + w_in_term, totals[1] + w_out_term), emb_grad)
    start = (jnp.zeros((D, 4 * HW), jnp.float32), jnp.zeros((D, HW), jnp.float32))
    (w_in_grad, w_out_grad), emb_blocks = lax.scan(advance_block, start, (x_blocks, g_blocks, seq_lengths))
    emb_grad = emb_blocks.reshape(TOKENS, D)
    row_index = (owners[:, 0] * SLOTS + slots).astype(jnp.int32)
    row_grad = jax.ops.segment_sum(emb_grad.astype(jnp.float32), row_index, num_segments=TABLE)
    row_count = jax.ops.segment_sum(jnp.ones((TOKENS,), jnp.float32), row_index, num_segments=TABLE)
    new_rows, new_mom, new_var = row_adam(emb_rows, emb_mom, emb_var, row_grad, row_count)
    return (new_rows, new_mom, new_var, w_in_grad, w_out_grad)
```

```python
import functools

import jax
import jax.numpy as jnp
from jax import lax
from jax.experimental import pallas as pl
from jax.experimental.pallas import tpu as pltpu
from jax.sharding import PartitionSpec as P

HEADS = 4
HEAD_DIM = 64
HW = 256
MAXLEN = 256


norm_eps = 1e-06
beta_one = 0.9
beta_two = 0.99
learn_rate = 0.05
adam_eps = 1e-08
bias_one = 1.0 - 0.9**10
bias_two = 1.0 - 0.99**10


def layer_norm(values):
    average = jnp.mean(values, axis=-1, keepdims=True)
    centered = values - average
    spread = jnp.mean(centered * centered, axis=-1, keepdims=True)
    return centered * lax.rsqrt(spread + norm_eps)


def allowed_mask(lengths, tok_count):
    ends = jnp.stack([jnp.sum(lengths[: i + 1]) for i in range(lengths.shape[0])])
    position = jnp.arange(tok_count, dtype=jnp.int32)
    segment = jnp.sum((position[:, None] >= ends[None, :]).astype(jnp.int32), axis=1)
    same = segment[:, None] == segment[None, :]
    causal = position[None, :] <= position[:, None]
    return (same & causal).astype(jnp.float32)


def core(pre, allowed):
    tok_count = pre.shape[0]
    proj = jax.nn.silu(pre).astype(jnp.bfloat16)
    upart, vpart, qpart, kpart = jnp.split(proj, 4, axis=1)
    queries = qpart.reshape(tok_count, HEADS, HEAD_DIM)
    keys_part = kpart.reshape(tok_count, HEADS, HEAD_DIM)
    values_part = vpart.reshape(tok_count, HEADS, HEAD_DIM)
    scores = jnp.einsum(
        "thd,shd->hts", queries, keys_part, preferred_element_type=jnp.float32
    ) * HEAD_DIM ** (-0.5)
    weights = (jax.nn.silu(scores) * allowed[None] / MAXLEN).astype(jnp.bfloat16)
    attn = jnp.einsum(
        "hts,shd->thd", weights, values_part, preferred_element_type=jnp.float32
    ).reshape(tok_count, HW)
    return (layer_norm(attn) * upart.astype(jnp.float32)).astype(jnp.bfloat16)


def row_adam(rows_now, mom_now, var_now, grad, counts):
    touched = counts > 0.5
    mom_next = beta_one * mom_now + (1.0 - beta_one) * grad
    var_next = beta_two * var_now + (1.0 - beta_two) * jnp.mean(grad * grad, axis=1)
    advance = mom_next / bias_one / (jnp.sqrt(var_next / bias_two)[:, None] + adam_eps)
    rows_next = rows_now - learn_rate * advance
    return (
        jnp.where(touched[:, None], rows_next, rows_now),
        jnp.where(touched[:, None], mom_next, mom_now),
        jnp.where(touched, var_next, var_now),
    )


def local(tokens, out_grad, seq_lengths, owners, slots, w_in, w_out, emb_rows, emb_mom, emb_var):
    tok_count = tokens.shape[0]
    width = tokens.shape[1]
    allowed = allowed_mask(seq_lengths[0], tok_count)
    normed_exact, norm_back = jax.vjp(layer_norm, tokens.astype(jnp.float32))
    normed = normed_exact.astype(jnp.bfloat16)
    pre = jnp.dot(normed, w_in, preferred_element_type=jnp.float32)
    y_out, core_back = jax.vjp(lambda inner: core(inner, allowed), pre)
    y_grad = jnp.dot(out_grad, w_out, preferred_element_type=jnp.float32).astype(jnp.bfloat16)
    pre_grad_b = core_back(y_grad)[0].astype(jnp.bfloat16)
    normed_grad = lax.dot_general(
        pre_grad_b, w_in, (((1,), (1,)), ((), ())), preferred_element_type=jnp.float32
    )
    emb_grad = (norm_back(normed_grad)[0] + out_grad.astype(jnp.float32)).astype(jnp.bfloat16)
    contract = (((0,), (0,)), ((), ()))
    in_cols = w_in.shape[1]
    owner_count = lax.axis_size("rows")
    weight_share = lax.psum_scatter(
        jnp.concatenate(
            [
                lax.dot_general(normed, pre_grad_b, contract, preferred_element_type=jnp.float32),
                lax.dot_general(out_grad, y_out, contract, preferred_element_type=jnp.float32),
            ],
            axis=1,
        ),
        "rows",
        scatter_dimension=0,
        tiled=True,
    )
    weight_share = lax.psum(weight_share, "dp")
    w_in_grad = weight_share[:, :in_cols]
    w_out_grad = weight_share[:, in_cols:]
    capacity = max(2, 4 * tok_count // owner_count)
    buffer_rows = owner_count * capacity
    owner_of = owners[:, 0]
    position = jnp.arange(tok_count, dtype=jnp.int32)
    earlier = jnp.sum(
        ((owner_of[:, None] == owner_of[None, :]) & (position[None, :] < position[:, None])).astype(
            jnp.int32
        ),
        axis=1,
    )
    position_to = owner_of * capacity + earlier
    chosen = position_to[None, :] == jnp.arange(buffer_rows, dtype=jnp.int32)[:, None]
    outgoing = jnp.dot(
        chosen.astype(jnp.bfloat16), emb_grad, preferred_element_type=jnp.float32
    ).astype(jnp.bfloat16)
    outgoing = outgoing.reshape(owner_count, capacity, width)
    out_slots = (jnp.sum(jnp.where(chosen, slots[None, :] + 1, 0), axis=1) - 1).reshape(
        owner_count, capacity
    )
    arrived, arrived_slots = (
        lax.all_to_all(outgoing, "rows", split_axis=0, concat_axis=0, tiled=True),
        lax.all_to_all(out_slots, "rows", split_axis=0, concat_axis=0, tiled=True),
    )
    received = arrived.reshape(buffer_rows, width)
    got_slots = arrived_slots.reshape(buffer_rows)
    slot_count = emb_rows.shape[0]
    matches = got_slots[None, :] == jnp.arange(slot_count, dtype=jnp.int32)[:, None]
    grad_part = jnp.dot(matches.astype(jnp.bfloat16), received, preferred_element_type=jnp.float32)
    count_part = jnp.sum(matches.astype(jnp.float32), axis=1)
    grad_all, count_all = lax.psum((grad_part, count_part), "dp")
    new_rows, new_mom, new_var = row_adam(emb_rows, emb_mom, emb_var, grad_all, count_all)
    return (new_rows, new_mom, new_var, w_in_grad, w_out_grad)


BF16 = jnp.bfloat16
F32 = jnp.float32

AXES = {"core": ("dp", 1), "x": ("dp", 2), "y": ("rows", 1), "z1": ("rows", 2), "z2": ("rows", 4)}


class Part:
    def __init__(self, name, owner_rows, cols, halve, swap):
        self.name, self.cols, self.halve, self.swap = name, cols, halve, swap
        self.gather = [a for a in halve if AXES[a][0] == "dp"][::-1]
        self.height = owner_rows // 2 ** len(self.gather)
        self.stages = [("halve", a) for a in halve] + [("swap", a) for a in swap]
        self.stages += [("gather", a) for a in self.gather]

    def shapes(self):
        chunk = (self.height, self.cols)
        halves = len(self.halve)
        shapes = [(2,) * halves + chunk]
        for step in range(halves):
            shapes.append((2,) * (halves - step - 1) + chunk)
        shapes += [chunk] * len(self.swap)
        gathered = [(2,) * (k + 1) + chunk for k in range(len(self.gather))]
        arrive = [(2,) * (halves - step - 1) + chunk for step in range(halves)] + [chunk] * len(self.swap)
        return shapes + gathered, arrive


class Exchange:
    def __init__(self, part, bufs, arrive, send_sems, recv_sems, base, bit, peer):
        self.part, self.bufs, self.arrive = part, bufs, arrive
        self.send_sems, self.recv_sems, self.base = send_sems, recv_sems, base
        self.bit, self.peer = bit, peer
        self.stage, self.copy = 0, None

    def put(self, owner, inner, value):
        bits = {"y": owner % 2, "z1": owner // 2 % 2, "z2": owner // 4, **inner}
        self.bufs[0][tuple(bits[a] for a in self.part.halve)] = value

    def put_rows(self, value):
        dims, height = self.part.gather[::-1], self.part.height
        per_owner = height * 2 ** len(dims)
        for owner in range(8):
            for q in range(2 ** len(dims)):
                inner = {a: q // 2 ** (len(dims) - 1 - k) % 2 for k, a in enumerate(dims)}
                first = owner * per_owner + q * height
                self.put(owner, inner, value[first : first + height].astype(BF16))

    def start(self):
        kind, axis = self.part.stages[self.stage]
        here = self.bufs[self.stage]
        if kind == "halve":
            source, target = here.at[1 - self.bit[axis]], self.arrive[self.stage]
        elif kind == "swap":
            source, target = here, self.arrive[self.stage]
        else:
            later = self.bufs[self.stage + 1]
            later[self.bit[axis]] = here[...]
            source = target = later.at[self.bit[axis]]
        self.copy = pltpu.make_async_remote_copy(
            src_ref=source,
            dst_ref=target,
            send_sem=self.send_sems.at[self.base + self.stage],
            recv_sem=self.recv_sems.at[self.base + self.stage],
            device_id=self.peer[axis],
            device_id_type=pl.DeviceIdType.MESH,
        )
        self.copy.start()

    def step(self):
        if self.stage == len(self.part.stages):
            return
        kind, axis = self.part.stages[self.stage]
        self.copy.wait()
        if kind != "gather":
            mine = self.bufs[self.stage][self.bit[axis]] if kind == "halve" else self.bufs[self.stage][...]
            total = mine.astype(F32) + self.arrive[self.stage][...].astype(F32)
            self.bufs[self.stage + 1][...] = total.astype(BF16)
        self.stage += 1
        if self.stage < len(self.part.stages):
            self.start()

    def result(self):
        out = self.bufs[-1][...]
        return out.reshape(-1, self.part.cols).astype(F32)


def dot(a, b, dims=((1,), (0,))):
    return lax.dot_general(a, b, (dims, ((), ())), preferred_element_type=F32)


def norm_parts(values):
    average = jnp.mean(values, axis=-1, keepdims=True)
    centered = values - average
    spread = jnp.mean(centered * centered, axis=-1, keepdims=True)
    scale = lax.rsqrt(spread + norm_eps)
    return centered * scale, scale


def norm_back(grad, normed, scale):
    inner = jnp.mean(grad * normed, axis=-1, keepdims=True)
    return scale * (grad - jnp.mean(grad, axis=-1, keepdims=True) - normed * inner)


def sigmoid(values):
    return 0.5 * jnp.tanh(0.5 * values) + 0.5


def column_of(row, count):
    return jnp.broadcast_to(row, (count, count)).T[:, :1]


def parts_of(slots, w_rows):
    return [
        Part("count", 16, slots, ["y", "z1", "z2"], ["x", "core"]),
        Part("early", w_rows, 3 * HW, ["core", "y", "z1", "z2"], ["x"]),
        Part("late", w_rows, 2 * HW, ["core", "x", "z1", "z2", "y"], []),
        Part("rows_a", slots, 256, ["core", "y", "z1", "z2"], ["x"]),
        Part("rows_b", slots, 256, ["core", "x", "z1", "z2", "y"], []),
    ]


def fused_kernel(parts, lens, tokens, grads, index, w_in, w_out, rows, mom, var, *rest):
    new_rows, new_mom, new_var, w_in_out, w_out_out = rest[:5]
    rest = list(rest[5:])
    send_sems, recv_sems, normed_t, slope, wst, dst, fac = rest[:7]
    rest = rest[7:]
    tok, width = tokens.shape
    slots = rows.shape[0]
    owners = 8
    r, p = lax.axis_index("rows"), lax.axis_index("dp")
    bit, peer = {}, {}
    for axis, (name, unit) in AXES.items():
        at = r if name == "rows" else p
        bit[axis] = at // unit % 2
        other = at + unit - 2 * unit * bit[axis]
        peer[axis] = (other, p) if name == "rows" else (r, other)
    barrier = pltpu.get_barrier_semaphore()
    for axis in AXES:
        pl.semaphore_signal(barrier, inc=1, device_id=peer[axis], device_id_type=pl.DeviceIdType.MESH)
    pl.semaphore_wait(barrier, len(AXES))

    made, base = {}, 0
    for part in parts:
        shapes, arrive = part.shapes()
        bufs = [rest.pop(0) for _ in shapes]
        landing = [rest.pop(0) for _ in arrive]
        made[part.name] = Exchange(part, bufs, landing, send_sems, recv_sems, base, bit, peer)
        base += len(part.stages)
    count, early, late = made["count"], made["early"], made["late"]
    rows_a, rows_b = made["rows_a"], made["rows_b"]

    row_id = lax.broadcasted_iota(jnp.int32, (owners * slots, tok), 0)
    named = (row_id == index[...]).astype(F32).astype(BF16)
    counts = dot(jnp.ones((16, tok), BF16), named, ((1,), (1,)))
    for owner in range(owners):
        count.put(owner, {}, counts[:, owner * slots : (owner + 1) * slots].astype(BF16))
    count.start()

    exact, scale_in = norm_parts(tokens[...].astype(F32))
    normed = exact.astype(BF16)
    normed_t[...] = normed.T
    proj = []
    for k in range(4):
        pre = dot(normed, w_in[:, k * HW : (k + 1) * HW])
        gate = sigmoid(pre)
        proj.append((pre * gate).astype(BF16))
        slope[:, k * HW : (k + 1) * HW] = gate * (1.0 + pre * (1.0 - gate))
    upart, vpart, qpart, kpart = proj
    count.step()

    feature = lax.broadcasted_iota(jnp.int32, (1, HW), 1) // HEAD_DIM
    heads = [(feature == h).astype(F32).astype(BF16) for h in range(HEADS)]
    block = MAXLEN // 2
    spans = [(i * block, max(0, i - 2) * block, (i + 1) * block) for i in range(tok // block)]
    ends, total = [], 0
    for s in range(lens.shape[1]):
        total = total + lens[0, s]
        ends.append(total)

    def segment(position):
        return sum((position >= e).astype(jnp.int32) for e in ends)

    masks = []
    for at, low, high in spans:
        query = at + lax.broadcasted_iota(jnp.int32, (block, 1), 0)
        key = low + lax.broadcasted_iota(jnp.int32, (1, high - low), 1)
        masks.append((segment(query) == segment(key)) & (key <= query))
    attn_rows = [None] * len(spans)
    for h in range(HEADS):
        keys, vals = kpart * heads[h], vpart * heads[h]
        for i, (at, low, high) in enumerate(spans):
            scores = dot(qpart[at : at + block], keys[low:high], ((1,), (1,))) * HEAD_DIM ** (-0.5)
            gate = jnp.where(masks[i], sigmoid(scores), 0.0)
            mass = (scores * gate * (1.0 / MAXLEN)).astype(BF16)
            here = pl.ds(h * tok + at, block)
            if low > 0:
                wst[here, 0:low] = jnp.zeros((block, low), BF16)
                dst[here, 0:low] = jnp.zeros((block, low), BF16)
            if high < tok:
                wst[here, high:tok] = jnp.zeros((block, tok - high), BF16)
                dst[here, high:tok] = jnp.zeros((block, tok - high), BF16)
            wst[here, low:high] = mass
            fac[here, low:high] = gate * (1.0 + scores * (1.0 - sigmoid(scores))) * (HEAD_DIM ** (-0.5) / MAXLEN)
            piece = dot(mass, vals[low:high])
            attn_rows[i] = piece if attn_rows[i] is None else attn_rows[i] + piece
        count.step()
    attn_hat, scale_mid = norm_parts(jnp.concatenate(attn_rows, axis=0))
    gate_u = upart.astype(F32)
    y_out = (attn_hat * gate_u).astype(BF16)

    y_grad = dot(grads[...], w_out[...]).astype(BF16).astype(F32)
    u_grad = (y_grad * attn_hat).astype(BF16).astype(F32)
    attn_grad = norm_back(y_grad * gate_u, attn_hat, scale_mid).astype(BF16)
    v_grad = 0.0
    for h in range(HEADS):
        v_grad = v_grad + dot(wst[h * tok : (h + 1) * tok, :], attn_grad * heads[h], ((0,), (0,)))
    pre_u = (u_grad * slope[:, :HW]).astype(BF16)
    pre_v = (v_grad.astype(BF16).astype(F32) * slope[:, HW : 2 * HW]).astype(BF16)
    early.put_rows(
        jnp.concatenate(
            [dot(grads[...].T, y_out), dot(normed_t[...], pre_u), dot(normed_t[...], pre_v)], axis=1
        )
    )
    early.start()
    q_rows = [None] * len(spans)
    k_grad = 0.0
    for h in range(HEADS):
        keys, vals, queries = kpart * heads[h], vpart * heads[h], qpart * heads[h]
        for i, (at, low, high) in enumerate(spans):
            here = pl.ds(h * tok + at, block)
            mass_grad = dot(attn_grad[at : at + block], vals[low:high], ((1,), (1,)))
            score_grad = (mass_grad.astype(BF16).astype(F32) * fac[here, low:high]).astype(BF16)
            dst[here, low:high] = score_grad
            piece = dot(score_grad, keys[low:high])
            q_rows[i] = piece if q_rows[i] is None else q_rows[i] + piece
        k_grad = k_grad + dot(dst[h * tok : (h + 1) * tok, :], queries, ((0,), (0,)))
        if h % 2 == 1:
            early.step()
    q_grad = jnp.concatenate(q_rows, axis=0)
    pre_q = (q_grad.astype(BF16).astype(F32) * slope[:, 2 * HW : 3 * HW]).astype(BF16)
    pre_k = (k_grad.astype(BF16).astype(F32) * slope[:, 3 * HW :]).astype(BF16)

    normed_grad = 0.0
    for k, piece in enumerate((pre_u, pre_v, pre_q, pre_k)):
        normed_grad = normed_grad + dot(piece, w_in[:, k * HW : (k + 1) * HW], ((1,), (1,)))
    exact, scale_in = norm_parts(tokens[...].astype(F32))
    emb_grad = (norm_back(normed_grad, exact, scale_in) + grads[...].astype(F32)).astype(BF16)
    rows_a.put_rows(dot(named, emb_grad[:, :256]))
    rows_a.start()
    rows_b.put_rows(dot(named, emb_grad[:, 256:]))
    rows_b.start()
    late.put_rows(jnp.concatenate([dot(normed_t[...], pre_q), dot(normed_t[...], pre_k)], axis=1))
    late.start()
    for _ in range(8):
        for exchange in (rows_a, rows_b, early, late, count):
            exchange.step()

    grad_a, grad_b = rows_a.result(), rows_b.result()
    touched = column_of(count.result()[:1], slots) > 0.5
    squares = jnp.sum(grad_a * grad_a, axis=1, keepdims=True) + jnp.sum(grad_b * grad_b, axis=1, keepdims=True)
    var_now = column_of(var[...], slots)
    var_next = beta_two * var_now + (1.0 - beta_two) * (squares * (1.0 / width))
    divisor = jnp.sqrt(var_next / bias_two) + adam_eps
    for at, grad in ((0, grad_a), (256, grad_b)):
        cols = slice(at, at + 256)
        mom_next = beta_one * mom[:, cols] + (1.0 - beta_one) * grad
        rows_next = rows[:, cols] - learn_rate * (mom_next / bias_one / divisor)
        new_rows[:, cols] = jnp.where(touched, rows_next, rows[:, cols])
        new_mom[:, cols] = jnp.where(touched, mom_next, mom[:, cols])
    var_out = jnp.where(touched, var_next, var_now)
    new_var[...] = jnp.broadcast_to(var_out, (slots, slots)).T[:1]
    out_early = early.result()
    w_out_out[...] = out_early[:, :HW]
    w_in_out[:, : 2 * HW] = out_early[:, HW:]
    w_in_out[:, 2 * HW :] = late.result()


def fused(tokens, out_grad, seq_lengths, owners, slots, w_in, w_out, emb_rows, emb_mom, emb_var):
    tok, width = tokens.shape
    count = emb_rows.shape[0]
    w_rows = w_in.shape[0] // lax.axis_size("rows")
    index = (owners.reshape(1, tok) * count + slots.reshape(1, tok)).astype(jnp.int32)
    parts = parts_of(count, w_rows)
    stages = sum(len(part.stages) for part in parts)
    scratch = [
        pltpu.SemaphoreType.DMA((stages,)),
        pltpu.SemaphoreType.DMA((stages,)),
        pltpu.VMEM((width, tok), BF16),
        pltpu.VMEM((tok, 4 * HW), F32),
        pltpu.VMEM((HEADS * tok, tok), BF16),
        pltpu.VMEM((HEADS * tok, tok), BF16),
        pltpu.VMEM((HEADS * tok, tok), F32),
    ]
    for part in parts:
        shapes, arrive = part.shapes()
        scratch += [pltpu.VMEM(shape, BF16) for shape in shapes + arrive]
    vmem = pl.BlockSpec(memory_space=pltpu.VMEM)
    new_rows, new_mom, new_var, w_in_grad, w_out_grad = pl.pallas_call(
        functools.partial(fused_kernel, parts),
        out_shape=(
            jax.ShapeDtypeStruct(emb_rows.shape, F32),
            jax.ShapeDtypeStruct(emb_mom.shape, F32),
            jax.ShapeDtypeStruct((1, count), F32),
            jax.ShapeDtypeStruct((w_rows, w_in.shape[1]), F32),
            jax.ShapeDtypeStruct((w_rows, w_out.shape[1]), F32),
        ),
        in_specs=[pl.BlockSpec(memory_space=pltpu.SMEM)] + [vmem] * 8,
        out_specs=[vmem] * 5,
        scratch_shapes=scratch,
        compiler_params=pltpu.CompilerParams(
            collective_id=0, has_side_effects=True, vmem_limit_bytes=56 * 2**20
        ),
    )(seq_lengths, tokens, out_grad, index, w_in, w_out, emb_rows, emb_mom, emb_var.reshape(1, count))
    return new_rows, new_mom, new_var.reshape(count), w_in_grad, w_out_grad


def solution(mesh):
    in_specs = (
        P(("rows", "dp"), None),
        P(("rows", "dp"), None),
        P(("rows", "dp"), None),
        P(("rows", "dp"), None),
        P(("rows", "dp")),
        P(),
        P(),
        P("rows", None),
        P("rows", None),
        P("rows"),
    )
    out_specs = (P("rows", None), P("rows", None), P("rows"), P("rows", None), P("rows", None))
    small = mesh.shape["rows"] == 8 and mesh.shape["dp"] == 4
    return jax.shard_map(fused if small else local, mesh=mesh, in_specs=in_specs, out_specs=out_specs, check_vma=False)
```

```python
import functools

import jax
import jax.numpy as jnp
from jax import lax
from jax.experimental import pallas as pl
from jax.experimental.pallas import tpu as pltpu
from jax.sharding import PartitionSpec as P

HEADS = 4
HEAD_DIM = 64
HW = 256
MAXLEN = 256


norm_eps = 1e-06
beta_one = 0.9
beta_two = 0.99
learn_rate = 0.05
adam_eps = 1e-08
bias_one = 1.0 - 0.9**10
bias_two = 1.0 - 0.99**10


def layer_norm(values):
    average = jnp.mean(values, axis=-1, keepdims=True)
    centered = values - average
    spread = jnp.mean(centered * centered, axis=-1, keepdims=True)
    return centered * lax.rsqrt(spread + norm_eps)


def allowed_mask(lengths, tok_count):
    ends = jnp.stack([jnp.sum(lengths[: i + 1]) for i in range(lengths.shape[0])])
    position = jnp.arange(tok_count, dtype=jnp.int32)
    segment = jnp.sum((position[:, None] >= ends[None, :]).astype(jnp.int32), axis=1)
    same = segment[:, None] == segment[None, :]
    causal = position[None, :] <= position[:, None]
    return (same & causal).astype(jnp.float32)


def core(pre, allowed):
    tok_count = pre.shape[0]
    proj = jax.nn.silu(pre).astype(jnp.bfloat16)
    upart, vpart, qpart, kpart = jnp.split(proj, 4, axis=1)
    queries = qpart.reshape(tok_count, HEADS, HEAD_DIM)
    keys_part = kpart.reshape(tok_count, HEADS, HEAD_DIM)
    values_part = vpart.reshape(tok_count, HEADS, HEAD_DIM)
    scores = jnp.einsum(
        "thd,shd->hts", queries, keys_part, preferred_element_type=jnp.float32
    ) * HEAD_DIM ** (-0.5)
    weights = (jax.nn.silu(scores) * allowed[None] / MAXLEN).astype(jnp.bfloat16)
    attn = jnp.einsum(
        "hts,shd->thd", weights, values_part, preferred_element_type=jnp.float32
    ).reshape(tok_count, HW)
    return (layer_norm(attn) * upart.astype(jnp.float32)).astype(jnp.bfloat16)


def row_adam(rows_now, mom_now, var_now, grad, counts):
    touched = counts > 0.5
    mom_next = beta_one * mom_now + (1.0 - beta_one) * grad
    var_next = beta_two * var_now + (1.0 - beta_two) * jnp.mean(grad * grad, axis=1)
    advance = mom_next / bias_one / (jnp.sqrt(var_next / bias_two)[:, None] + adam_eps)
    rows_next = rows_now - learn_rate * advance
    return (
        jnp.where(touched[:, None], rows_next, rows_now),
        jnp.where(touched[:, None], mom_next, mom_now),
        jnp.where(touched, var_next, var_now),
    )


def local(tokens, out_grad, seq_lengths, owners, slots, w_in, w_out, emb_rows, emb_mom, emb_var):
    tok_count = tokens.shape[0]
    width = tokens.shape[1]
    allowed = allowed_mask(seq_lengths[0], tok_count)
    normed_exact, norm_back = jax.vjp(layer_norm, tokens.astype(jnp.float32))
    normed = normed_exact.astype(jnp.bfloat16)
    pre = jnp.dot(normed, w_in, preferred_element_type=jnp.float32)
    y_out, core_back = jax.vjp(lambda inner: core(inner, allowed), pre)
    y_grad = jnp.dot(out_grad, w_out, preferred_element_type=jnp.float32).astype(jnp.bfloat16)
    pre_grad_b = core_back(y_grad)[0].astype(jnp.bfloat16)
    normed_grad = lax.dot_general(
        pre_grad_b, w_in, (((1,), (1,)), ((), ())), preferred_element_type=jnp.float32
    )
    emb_grad = (norm_back(normed_grad)[0] + out_grad.astype(jnp.float32)).astype(jnp.bfloat16)
    contract = (((0,), (0,)), ((), ()))
    in_cols = w_in.shape[1]
    owner_count = lax.axis_size("rows")
    weight_share = lax.psum_scatter(
        jnp.concatenate(
            [
                lax.dot_general(normed, pre_grad_b, contract, preferred_element_type=jnp.float32),
                lax.dot_general(out_grad, y_out, contract, preferred_element_type=jnp.float32),
            ],
            axis=1,
        ),
        "rows",
        scatter_dimension=0,
        tiled=True,
    )
    weight_share = lax.psum(weight_share, "dp")
    w_in_grad = weight_share[:, :in_cols]
    w_out_grad = weight_share[:, in_cols:]
    capacity = max(2, 4 * tok_count // owner_count)
    buffer_rows = owner_count * capacity
    owner_of = owners[:, 0]
    position = jnp.arange(tok_count, dtype=jnp.int32)
    earlier = jnp.sum(
        ((owner_of[:, None] == owner_of[None, :]) & (position[None, :] < position[:, None])).astype(
            jnp.int32
        ),
        axis=1,
    )
    position_to = owner_of * capacity + earlier
    chosen = position_to[None, :] == jnp.arange(buffer_rows, dtype=jnp.int32)[:, None]
    outgoing = jnp.dot(
        chosen.astype(jnp.bfloat16), emb_grad, preferred_element_type=jnp.float32
    ).astype(jnp.bfloat16)
    outgoing = outgoing.reshape(owner_count, capacity, width)
    out_slots = (jnp.sum(jnp.where(chosen, slots[None, :] + 1, 0), axis=1) - 1).reshape(
        owner_count, capacity
    )
    arrived, arrived_slots = (
        lax.all_to_all(outgoing, "rows", split_axis=0, concat_axis=0, tiled=True),
        lax.all_to_all(out_slots, "rows", split_axis=0, concat_axis=0, tiled=True),
    )
    received = arrived.reshape(buffer_rows, width)
    got_slots = arrived_slots.reshape(buffer_rows)
    slot_count = emb_rows.shape[0]
    matches = got_slots[None, :] == jnp.arange(slot_count, dtype=jnp.int32)[:, None]
    grad_part = jnp.dot(matches.astype(jnp.bfloat16), received, preferred_element_type=jnp.float32)
    count_part = jnp.sum(matches.astype(jnp.float32), axis=1)
    grad_all, count_all = lax.psum((grad_part, count_part), "dp")
    new_rows, new_mom, new_var = row_adam(emb_rows, emb_mom, emb_var, grad_all, count_all)
    return (new_rows, new_mom, new_var, w_in_grad, w_out_grad)


BF16 = jnp.bfloat16
F32 = jnp.float32

CUTS = {"core": 2, "x": 2, "y": 2, "z": 4, "rows": 8}


class Part:
    def __init__(self, name, owner_rows, cols, cuts, last):
        self.name, self.cols, self.cuts, self.last = name, cols, cuts, last
        self.inner = [c for c in cuts if c in ("core", "x")]
        self.height = owner_rows // 2 ** len(self.inner)
        self.moves = [CUTS[c] - 1 for c in cuts] + [3]

    def shapes(self):
        chunk = (self.height, self.cols)
        sizes = [CUTS[c] for c in self.cuts]
        bufs = [tuple(sizes[k:]) + chunk for k in range(len(sizes) + 1)]
        arrive = [(n - 1,) + bufs[k + 1] for k, n in enumerate(sizes)]
        last = (4,) + chunk if self.last == "gather" else (3,) + chunk
        return bufs, arrive + [last]


class Exchange:
    def __init__(self, part, bufs, arrive, send_sems, recv_sems, base, place):
        self.part, self.bufs, self.arrive = part, bufs, arrive
        self.send_sems, self.recv_sems, self.base = send_sems, recv_sems, base
        self.place, self.stage, self.copies = place, 0, []

    def put(self, owner, inner, value):
        at = {"y": owner % 2, "z": owner // 2, "rows": owner, **inner}
        self.bufs[0][tuple(at[c] for c in self.part.cuts)] = value

    def put_rows(self, value):
        names, height = self.part.inner, self.part.height
        per_owner = height * 2 ** len(names)
        for owner in range(8):
            for q in range(2 ** len(names)):
                inner = {c: q // 2 ** (len(names) - 1 - k) % 2 for k, c in enumerate(names)}
                first = owner * per_owner + q * height
                self.put(owner, inner, value[first : first + height].astype(BF16))

    def start(self):
        here, landing = self.bufs[self.stage], self.arrive[self.stage]
        self.copies = []
        if self.stage < len(self.part.cuts):
            at, takers = self.place[self.part.cuts[self.stage]]
            moves = [(here.at[where], landing.at[k], device) for k, (where, device) in enumerate(takers)]
        else:
            block, peers = self.place["dp"]
            if self.part.last == "gather":
                landing[block] = here[...]
                moves = [(landing.at[block], landing.at[block], device) for device in peers]
            else:
                moves = [(here, landing.at[k], device) for k, device in enumerate(peers)]
        for k, (source, target, device) in enumerate(moves):
            copy = pltpu.make_async_remote_copy(
                src_ref=source,
                dst_ref=target,
                send_sem=self.send_sems.at[self.base + k],
                recv_sem=self.recv_sems.at[self.base + k],
                device_id=device,
                device_id_type=pl.DeviceIdType.MESH,
            )
            copy.start()
            self.copies.append(copy)

    def step(self):
        if self.stage == len(self.part.moves):
            return
        for copy in self.copies:
            copy.wait()
        if self.stage < len(self.part.cuts):
            at, _ = self.place[self.part.cuts[self.stage]]
            total = self.bufs[self.stage][at].astype(F32)
            for k in range(self.part.moves[self.stage]):
                total = total + self.arrive[self.stage][k].astype(F32)
            self.bufs[self.stage + 1][...] = total.astype(BF16)
        self.base += self.part.moves[self.stage]
        self.stage += 1
        if self.stage < len(self.part.moves):
            self.start()

    def result(self):
        here, landing = self.bufs[-1], self.arrive[-1]
        if self.part.last == "gather":
            return landing[...].reshape(-1, self.part.cols).astype(F32)
        by_core, by_x, by_both = (landing[k].astype(F32) for k in range(3))
        mine, other = here[...].astype(F32) + by_x, by_core + by_both
        if self.part.last == "sum":
            return mine + other
        first = self.place["core"][0] == 0
        return jnp.concatenate([jnp.where(first, mine, other), jnp.where(first, other, mine)], axis=0)


def dot(a, b, dims=((1,), (0,))):
    return lax.dot_general(a, b, (dims, ((), ())), preferred_element_type=F32)


def norm_parts(values):
    average = jnp.mean(values, axis=-1, keepdims=True)
    centered = values - average
    spread = jnp.mean(centered * centered, axis=-1, keepdims=True)
    scale = lax.rsqrt(spread + norm_eps)
    return centered * scale, scale


def norm_back(grad, normed, scale):
    inner = jnp.mean(grad * normed, axis=-1, keepdims=True)
    return scale * (grad - jnp.mean(grad, axis=-1, keepdims=True) - normed * inner)


def sigmoid(values):
    return 0.5 * jnp.tanh(0.5 * values) + 0.5


def column_of(row, count):
    return jnp.broadcast_to(row, (count, count)).T[:, :1]


def parts_of(slots, w_rows):
    return [
        Part("count", 16, slots, ["y", "z"], "sum"),
        Part("early", w_rows, 3 * HW, ["core", "x", "rows"], "gather"),
        Part("late", w_rows, 2 * HW, ["core", "y", "z"], "pair"),
        Part("rows_a", slots, 256, ["core", "y", "z"], "pair"),
        Part("rows_b", slots, 256, ["core", "x", "rows"], "gather"),
    ]


def fused_kernel(parts, lens, tokens, grads, index, w_in, w_out, rows, mom, var, *rest):
    new_rows, new_mom, new_var, w_in_out, w_out_out = rest[:5]
    rest = list(rest[5:])
    send_sems, recv_sems, normed_t, slope, wst, dst, fac = rest[:7]
    rest = rest[7:]
    tok, width = tokens.shape
    slots = rows.shape[0]
    owners = 8
    r, p = lax.axis_index("rows"), lax.axis_index("dp")
    core, x, y, z = p % 2, p // 2, r % 2, r // 2
    by_core, by_x = (r, p + 1 - 2 * core), (r, p + 2 - 4 * x)
    by_both, by_y = (r, 3 - p), (r + 1 - 2 * y, p)
    by_rows = [lax.rem(r + k, owners) for k in range(1, owners)]
    place = {
        "core": (core, [(1 - core, by_core)]),
        "x": (x, [(1 - x, by_x)]),
        "y": (y, [(1 - y, by_y)]),
        "z": (z, [(by_rows[2 * k - 1] // 2, (by_rows[2 * k - 1], p)) for k in (1, 2, 3)]),
        "rows": (r, [(to, (to, p)) for to in by_rows]),
        "dp": (core * 2 + x, [by_core, by_x, by_both]),
    }
    barrier = pltpu.get_barrier_semaphore()
    greeted = [by_core, by_x, by_both] + [(to, p) for to in by_rows]
    for device in greeted:
        pl.semaphore_signal(barrier, inc=1, device_id=device, device_id_type=pl.DeviceIdType.MESH)
    pl.semaphore_wait(barrier, len(greeted))

    made, base = {}, 0
    for part in parts:
        shapes, arrive = part.shapes()
        bufs = [rest.pop(0) for _ in shapes]
        landing = [rest.pop(0) for _ in arrive]
        made[part.name] = Exchange(part, bufs, landing, send_sems, recv_sems, base, place)
        base += sum(part.moves)
    count, early, late = made["count"], made["early"], made["late"]
    rows_a, rows_b = made["rows_a"], made["rows_b"]

    row_id = lax.broadcasted_iota(jnp.int32, (owners * slots, tok), 0)
    named = (row_id == index[...]).astype(F32).astype(BF16)
    counts = dot(jnp.ones((16, tok), BF16), named, ((1,), (1,)))
    for owner in range(owners):
        count.put(owner, {}, counts[:, owner * slots : (owner + 1) * slots].astype(BF16))
    count.start()

    exact, scale_in = norm_parts(tokens[...].astype(F32))
    normed = exact.astype(BF16)
    normed_t[...] = normed.T
    proj = []
    for k in range(4):
        pre = dot(normed, w_in[:, k * HW : (k + 1) * HW])
        gate = sigmoid(pre)
        proj.append((pre * gate).astype(BF16))
        slope[:, k * HW : (k + 1) * HW] = gate * (1.0 + pre * (1.0 - gate))
    upart, vpart, qpart, kpart = proj

    feature = lax.broadcasted_iota(jnp.int32, (1, HW), 1) // HEAD_DIM
    heads = [(feature == h).astype(F32).astype(BF16) for h in range(HEADS)]
    block = MAXLEN // 2
    spans = [(i * block, max(0, i - 2) * block, (i + 1) * block) for i in range(tok // block)]
    ends, total = [], 0
    for s in range(lens.shape[1]):
        total = total + lens[0, s]
        ends.append(total)

    def segment(position):
        return sum((position >= e).astype(jnp.int32) for e in ends)

    masks = []
    for at, low, high in spans:
        query = at + lax.broadcasted_iota(jnp.int32, (block, 1), 0)
        key = low + lax.broadcasted_iota(jnp.int32, (1, high - low), 1)
        masks.append((segment(query) == segment(key)) & (key <= query))
    attn_rows = [None] * len(spans)
    for h in range(HEADS):
        keys, vals = kpart * heads[h], vpart * heads[h]
        for i, (at, low, high) in enumerate(spans):
            scores = dot(qpart[at : at + block], keys[low:high], ((1,), (1,))) * HEAD_DIM ** (-0.5)
            gate = jnp.where(masks[i], sigmoid(scores), 0.0)
            mass = (scores * gate * (1.0 / MAXLEN)).astype(BF16)
            here = pl.ds(h * tok + at, block)
            if low > 0:
                wst[here, 0:low] = jnp.zeros((block, low), BF16)
                dst[here, 0:low] = jnp.zeros((block, low), BF16)
            if high < tok:
                wst[here, high:tok] = jnp.zeros((block, tok - high), BF16)
                dst[here, high:tok] = jnp.zeros((block, tok - high), BF16)
            wst[here, low:high] = mass
            fac[here, low:high] = gate * (1.0 + scores * (1.0 - sigmoid(scores))) * (HEAD_DIM ** (-0.5) / MAXLEN)
            piece = dot(mass, vals[low:high])
            attn_rows[i] = piece if attn_rows[i] is None else attn_rows[i] + piece
    attn_hat, scale_mid = norm_parts(jnp.concatenate(attn_rows, axis=0))
    gate_u = upart.astype(F32)
    y_out = (attn_hat * gate_u).astype(BF16)

    y_grad = dot(grads[...], w_out[...]).astype(BF16).astype(F32)
    u_grad = (y_grad * attn_hat).astype(BF16).astype(F32)
    attn_grad = norm_back(y_grad * gate_u, attn_hat, scale_mid).astype(BF16)
    v_grad = 0.0
    for h in range(HEADS):
        v_grad = v_grad + dot(wst[h * tok : (h + 1) * tok, :], attn_grad * heads[h], ((0,), (0,)))
    pre_u = (u_grad * slope[:, :HW]).astype(BF16)
    pre_v = (v_grad.astype(BF16).astype(F32) * slope[:, HW : 2 * HW]).astype(BF16)
    early.put_rows(
        jnp.concatenate(
            [dot(grads[...].T, y_out), dot(normed_t[...], pre_u), dot(normed_t[...], pre_v)], axis=1
        )
    )
    early.start()
    q_rows = [None] * len(spans)
    k_grad = 0.0
    for h in range(HEADS):
        keys, vals, queries = kpart * heads[h], vpart * heads[h], qpart * heads[h]
        for i, (at, low, high) in enumerate(spans):
            here = pl.ds(h * tok + at, block)
            mass_grad = dot(attn_grad[at : at + block], vals[low:high], ((1,), (1,)))
            score_grad = (mass_grad.astype(BF16).astype(F32) * fac[here, low:high]).astype(BF16)
            dst[here, low:high] = score_grad
            piece = dot(score_grad, keys[low:high])
            q_rows[i] = piece if q_rows[i] is None else q_rows[i] + piece
        k_grad = k_grad + dot(dst[h * tok : (h + 1) * tok, :], queries, ((0,), (0,)))
        if h % 2 == 1:
            early.step()
            count.step()
    q_grad = jnp.concatenate(q_rows, axis=0)
    pre_q = (q_grad.astype(BF16).astype(F32) * slope[:, 2 * HW : 3 * HW]).astype(BF16)
    pre_k = (k_grad.astype(BF16).astype(F32) * slope[:, 3 * HW :]).astype(BF16)

    normed_grad = 0.0
    for k, piece in enumerate((pre_u, pre_v, pre_q, pre_k)):
        normed_grad = normed_grad + dot(piece, w_in[:, k * HW : (k + 1) * HW], ((1,), (1,)))
    exact, scale_in = norm_parts(tokens[...].astype(F32))
    emb_grad = (norm_back(normed_grad, exact, scale_in) + grads[...].astype(F32)).astype(BF16)
    rows_a.put_rows(dot(named, emb_grad[:, :256]))
    rows_a.start()
    rows_b.put_rows(dot(named, emb_grad[:, 256:]))
    rows_b.start()
    late.put_rows(jnp.concatenate([dot(normed_t[...], pre_q), dot(normed_t[...], pre_k)], axis=1))
    late.start()
    for _ in range(4):
        for exchange in (early, rows_a, rows_b, late, count):
            exchange.step()

    grad_a, grad_b = rows_a.result(), rows_b.result()
    touched = column_of(count.result()[:1], slots) > 0.5
    squares = jnp.sum(grad_a * grad_a, axis=1, keepdims=True) + jnp.sum(grad_b * grad_b, axis=1, keepdims=True)
    var_now = column_of(var[...], slots)
    var_next = beta_two * var_now + (1.0 - beta_two) * (squares * (1.0 / width))
    divisor = jnp.sqrt(var_next / bias_two) + adam_eps
    for at, grad in ((0, grad_a), (256, grad_b)):
        cols = slice(at, at + 256)
        mom_next = beta_one * mom[:, cols] + (1.0 - beta_one) * grad
        rows_next = rows[:, cols] - learn_rate * (mom_next / bias_one / divisor)
        new_rows[:, cols] = jnp.where(touched, rows_next, rows[:, cols])
        new_mom[:, cols] = jnp.where(touched, mom_next, mom[:, cols])
    var_out = jnp.where(touched, var_next, var_now)
    new_var[...] = jnp.broadcast_to(var_out, (slots, slots)).T[:1]
    out_early = early.result()
    w_out_out[...] = out_early[:, :HW]
    w_in_out[:, : 2 * HW] = out_early[:, HW:]
    w_in_out[:, 2 * HW :] = late.result()


def fused(tokens, out_grad, seq_lengths, owners, slots, w_in, w_out, emb_rows, emb_mom, emb_var):
    tok, width = tokens.shape
    count = emb_rows.shape[0]
    w_rows = w_in.shape[0] // lax.axis_size("rows")
    index = (owners.reshape(1, tok) * count + slots.reshape(1, tok)).astype(jnp.int32)
    parts = parts_of(count, w_rows)
    stages = sum(sum(part.moves) for part in parts)
    scratch = [
        pltpu.SemaphoreType.DMA((stages,)),
        pltpu.SemaphoreType.DMA((stages,)),
        pltpu.VMEM((width, tok), BF16),
        pltpu.VMEM((tok, 4 * HW), F32),
        pltpu.VMEM((HEADS * tok, tok), BF16),
        pltpu.VMEM((HEADS * tok, tok), BF16),
        pltpu.VMEM((HEADS * tok, tok), F32),
    ]
    for part in parts:
        shapes, arrive = part.shapes()
        scratch += [pltpu.VMEM(shape, BF16) for shape in shapes + arrive]
    vmem = pl.BlockSpec(memory_space=pltpu.VMEM)
    new_rows, new_mom, new_var, w_in_grad, w_out_grad = pl.pallas_call(
        functools.partial(fused_kernel, parts),
        out_shape=(
            jax.ShapeDtypeStruct(emb_rows.shape, F32),
            jax.ShapeDtypeStruct(emb_mom.shape, F32),
            jax.ShapeDtypeStruct((1, count), F32),
            jax.ShapeDtypeStruct((w_rows, w_in.shape[1]), F32),
            jax.ShapeDtypeStruct((w_rows, w_out.shape[1]), F32),
        ),
        in_specs=[pl.BlockSpec(memory_space=pltpu.SMEM)] + [vmem] * 8,
        out_specs=[vmem] * 5,
        scratch_shapes=scratch,
        compiler_params=pltpu.CompilerParams(
            collective_id=0, has_side_effects=True, vmem_limit_bytes=56 * 2**20
        ),
    )(seq_lengths, tokens, out_grad, index, w_in, w_out, emb_rows, emb_mom, emb_var.reshape(1, count))
    return new_rows, new_mom, new_var.reshape(count), w_in_grad, w_out_grad


def solution(mesh):
    in_specs = (
        P(("rows", "dp"), None),
        P(("rows", "dp"), None),
        P(("rows", "dp"), None),
        P(("rows", "dp"), None),
        P(("rows", "dp")),
        P(),
        P(),
        P("rows", None),
        P("rows", None),
        P("rows"),
    )
    out_specs = (P("rows", None), P("rows", None), P("rows"), P("rows", None), P("rows", None))
    small = mesh.shape["rows"] == 8 and mesh.shape["dp"] == 4
    return jax.shard_map(fused if small else local, mesh=mesh, in_specs=in_specs, out_specs=out_specs, check_vma=False)
```
